768 devices in a mesh: ext: 192 (over x_lo, z, y), pair: 4 (over x_hi, core).
Axes of the slice: x: 4 (x_hi: 2, x_lo: 2; x = x_hi * 2 + x_lo), y: 8, z: 12, core: 2. Of those that a mesh axis runs over, the one named last changes fastest.
Arguments:
- core_coef: bfloat16 [1536, 3072], P('ext', 'pair'), may hold values from -6 to 6
- dest_rows: int32 [192, 1536], P('ext'), may hold values from 0 to 255
- block_ids: int32 [192, 1536], P('ext'), may hold values from 0 to 1
- bin_offsets: int32 [192, 192], P('ext'), may hold values from 1 to 8, as said below
- couplings: bfloat16 [2, 3072, 3072], P(None, 'pair'), may hold values from -0.109375 to 0.109375
- energy_gap: float32 [49152, 3072], P('ext', 'pair'), may hold values from 0.5 to 5
Outputs:
- numerators: float32 [49152, 3072], P('ext', 'pair')
- energies: float32 [49152, 3072], P('ext', 'pair')
The draws below stay inside these ranges and needn't reach their ends.
Inputs may be any that keep to these rules, and one draw needn't show every extreme that they name: bin_offsets[d, d] = 8 for every d.
All inputs are finite; a program needn't handle non-finite values.
Results may differ from the reference program's by a relative error of at most 0.0033.
Values may be sent and summed in bfloat16 or wider, within the bound.
No kernel may reach another device: no remote copies, remote signals or barrier semaphores. Data moves between devices by JAX's collectives and lax.ppermute only.
A program may use at most 64 MiB of HBM per device.

```python
import math
import jax
import jax.numpy as jnp
from jax import lax

NB = 3072
NQ = 2
CH = 8
TILE = 256
NCORE = 1536
NEXT = 49152
N_EXT = 192


def draw_bin_offsets(key, part):
    key = jax.random.fold_in(key, 11)
    cuts = jax.random.randint(key, (N_EXT, N_EXT), 1, CH + 1)
    tiles = jnp.arange(N_EXT, dtype=jnp.int32)
    diagonal = tiles[:, None] == tiles[None, :]
    return jnp.where(diagonal, CH, cuts).astype(jnp.int32)


def place_ends(drawn, own_key, smallest, largest):
    index_at = [jax.random.randint(jax.random.fold_in(own_key, axis), (), 0, length) for axis, length in enumerate(drawn.shape)]
    longest = drawn.shape.index(max(drawn.shape))
    beside = index_at[:longest] + [(index_at[longest] + 1) % drawn.shape[longest]] + index_at[longest + 1:]
    return drawn.at[tuple(index_at)].set(smallest).at[tuple(beside)].set(largest)


def block_levels(stream_key, extent, pieces, least, largest):
    def one(position, blocks):
        draws = jax.random.uniform(jax.random.fold_in(jax.random.fold_in(stream_key, 6), position), (blocks,), jnp.float32, least / len(pieces), largest / len(pieces))
        return jnp.repeat(jnp.exp(draws), extent[position] // blocks).reshape((-1,) + (1,) * (len(extent) - position - 1))

    gain = one(*pieces[0])
    for cut in pieces[1:]:
        gain = gain * one(*cut)
    return gain


def gaussian(stream_key, extent, spread, most, cuts=(), kind=jnp.bfloat16):
    loudness = block_levels(stream_key, extent, cuts, -0.22, 0.18) if cuts else 1.0
    entries = jax.random.normal(stream_key, extent, jnp.float32) * spread * loudness
    return jnp.minimum(jnp.maximum(entries, -most), most).astype(kind)


def setup_inputs(seed: int = 0) -> dict:
    key_list = jax.random.split(jax.random.key(seed), 7)
    return {
        "core_coef": gaussian(key_list[0], (NCORE, NB), 1.0, 6.0, ((0, 192), (1, 4))),
        "dest_rows": place_ends(jax.random.randint(key_list[1], (N_EXT, NCORE), 0, TILE), jax.random.fold_in(key_list[1], 1), 0, TILE - 1).astype(jnp.int32),
        "block_ids": place_ends(jax.random.randint(key_list[2], (N_EXT, NCORE), 0, NQ), jax.random.fold_in(key_list[2], 1), 0, NQ - 1).astype(jnp.int32),
        "bin_offsets": draw_bin_offsets(jax.random.fold_in(key_list[6], 71), 0),
        "couplings": gaussian(key_list[4], (NQ, NB, NB), NB ** -0.5, 0.109375, ((1, 4),)),
        "energy_gap": jnp.clip(jnp.exp(math.log(5.0) - 2.3025851 * jax.random.uniform(key_list[5], (NEXT, NB), jnp.float32) ** block_levels(key_list[5], (NEXT, NB), ((0, 192), (1, 4)), -0.2, 0.2)), 0.5, 5.0),
    }


def reference(core_coef, dest_rows, block_ids, bin_offsets, couplings, energy_gap):
    coef_wide = core_coef.astype(jnp.float32)
    strings = jnp.arange(NCORE, dtype=jnp.int32)
    source_of = (strings // CH).astype(jnp.int32)
    within = (strings % CH).astype(jnp.int32)

    def one_tile(tile_maps):
        row_map, block_map, screen = tile_maps
        cut_for = screen[source_of]
        slot_index = jnp.where(within < cut_for, block_map * TILE + row_map, NQ * TILE).astype(jnp.int32)
        summed = jax.ops.segment_sum(coef_wide, slot_index, num_segments=NQ * TILE + 1)
        return summed[: NQ * TILE].reshape(NQ, TILE, NB).astype(jnp.bfloat16)

    gathered = lax.map(one_tile, (dest_rows, block_ids, bin_offsets))
    numerators = jnp.zeros((NEXT, NB), jnp.float32)
    for block_idx in range(NQ):
        block_rows = gathered[:, block_idx].reshape(NEXT, NB)
        numerators = numerators + jnp.dot(block_rows, couplings[block_idx], preferred_element_type=jnp.float32)
    energies = -(numerators * numerators) / energy_gap
    return numerators, energies
```

```python
import jax
import jax.numpy as jnp
from jax import lax
from jax.sharding import Mesh
from jax.sharding import PartitionSpec as P

NAMES = ("xl", "zh", "zl", "yh", "yl", "xh", "c")
SIZES = (2, 4, 3, 4, 2, 2, 2)
EXT = NAMES[:5]
FAR = ("xl", "zh", "yh")
NEAR = ((1, 1), (-1, -1), (1, 0), (-1, 0), (0, 1))


def shift(dz, dy):
    pairs = []
    for x in range(2):
        for z in range(12):
            for y in range(8):
                pairs.append(((x * 12 + z) * 8 + y, (x * 12 + (z + dz) % 12) * 8 + (y + dy) % 8))
    return pairs


def shards(core_coef, dest_rows, block_ids, bin_offsets, couplings, energy_gap):
    zl, yl = lax.axis_index("zl"), lax.axis_index("yl")
    xh, c = lax.axis_index("xh"), lax.axis_index("c")
    group_rows, width = core_coef.shape
    tile_rows = energy_gap.shape[0]
    spread = jnp.broadcast_to(core_coef[None], (32, group_rows, width))
    own = lax.all_to_all(spread, FAR, 0, 0, tiled=True).reshape(256, width)
    pieces = [own] + [lax.ppermute(own, EXT, shift(*at)) for at in NEAR]

    within = jnp.arange(8, dtype=jnp.int32)
    target = jnp.where(
        within[None, :] < bin_offsets[0][:, None],
        block_ids[0].reshape(192, 8) * tile_rows + dest_rows[0].reshape(192, 8),
        -1,
    )
    target = target.reshape(2, 4, 3, 4, 2, 8).transpose(2, 4, 0, 1, 3, 5).reshape(3, 2, 256)
    slots = jnp.arange(2 * tile_rows, dtype=jnp.int32)
    summed = jnp.zeros((2 * tile_rows, width), jnp.float32)
    for (dz, dy), piece in zip(((0, 0),) + NEAR, pieces):
        row = target[(zl - dz) % 3, (yl - dy) % 2]
        onehot = (slots[:, None] == row[None, :]).astype(jnp.bfloat16)
        summed = summed + jnp.dot(onehot, piece, preferred_element_type=jnp.float32)
    gathered = summed.astype(jnp.bfloat16).reshape(2, tile_rows, width)

    partial = jnp.einsum("qtb,qbc->tc", gathered, couplings, preferred_element_type=jnp.float32)
    swap = [(0, 1), (1, 0)]

    def columns(h, k):
        return lax.dynamic_slice_in_dim(partial, (h * 2 + k) * width, width, 1)

    far_in = lax.ppermute(columns(1 - xh, 1 - c).astype(jnp.bfloat16), "c", swap)
    far = (columns(1 - xh, c) + far_in.astype(jnp.float32)).astype(jnp.bfloat16)
    far = lax.ppermute(far, "xh", swap)
    near_in = lax.ppermute(columns(xh, 1 - c).astype(jnp.bfloat16), "c", swap)
    numerators = columns(xh, c) + near_in.astype(jnp.float32) + far.astype(jnp.float32)
    energies = -(numerators * numerators) / energy_gap
    return (numerators, energies)


def solution(mesh):
    fine = Mesh(mesh.devices.reshape(SIZES), NAMES)
    ext, pair = EXT, NAMES[5:]
    in_specs = (
        P(ext, pair),
        P(ext, None),
        P(ext, None),
        P(ext, None),
        P(None, pair, None),
        P(ext, pair),
    )
    out_specs = (P(ext, pair), P(ext, pair))
    return jax.shard_map(shards, mesh=fine, in_specs=in_specs, out_specs=out_specs, check_vma=False)
```

```python
import jax
import jax.numpy as jnp
from jax import lax
from jax.sharding import Mesh
from jax.sharding import PartitionSpec as P

NAMES = ("xl", "zh", "zl", "yh", "yl", "xh", "c")
SIZES = (2, 6, 2, 4, 2, 2, 2)
EXT = NAMES[:5]
FAR = ("zh", "yh")
NEAR = ((1, 1), (1, 0), (0, 1))
SWAP = [(0, 1), (1, 0)]


def shift(dx, dz, dy):
    pairs = []
    for x in range(2):
        for z in range(12):
            for y in range(8):
                for k in range(4):
                    s = -1 if k % 2 else 1
                    there = (((x + dx) % 2) * 12 + (z + s * dz) % 12) * 8 + (y + s * dy) % 8
                    pairs.append((((x * 12 + z) * 8 + y) * 4 + k, there * 4 + k))
    return pairs


def shards(core_coef, dest_rows, block_ids, bin_offsets, couplings, energy_gap):
    xl, zl, yl = lax.axis_index("xl"), lax.axis_index("zl"), lax.axis_index("yl")
    xh, c = lax.axis_index("xh"), lax.axis_index("c")
    group_rows, width = core_coef.shape
    tile_rows = energy_gap.shape[0]
    spread = jnp.broadcast_to(core_coef[None], (24, group_rows, width))
    own = lax.all_to_all(spread, FAR, 0, 0, tiled=True).reshape(192, width)
    beside = lax.ppermute(own, NAMES, shift(1, 0, 0))
    pieces = [((0, 0, 0), own)]
    pieces += [((0,) + at, lax.ppermute(own, NAMES, shift(0, *at))) for at in NEAR]
    pieces += [((1, 0, 0), beside)]
    pieces += [((1,) + at, lax.ppermute(beside, NAMES, shift(0, *at))) for at in NEAR]

    within = jnp.arange(8, dtype=jnp.int32)
    target = jnp.where(
        within[None, :] < bin_offsets[0][:, None],
        block_ids[0].reshape(192, 8) * tile_rows + dest_rows[0].reshape(192, 8),
        -1,
    )
    target = target.reshape(2, 6, 2, 4, 2, 8).transpose(0, 2, 4, 1, 3, 5).reshape(2, 2, 2, 192)
    slots = jnp.arange(2 * tile_rows, dtype=jnp.int32)
    summed = jnp.zeros((2 * tile_rows, width), jnp.float32)
    for (dx, dz, dy), piece in pieces:
        row = target[(xl + dx) % 2, (zl + dz) % 2, (yl + dy) % 2]
        onehot = (slots[:, None] == row[None, :]).astype(jnp.bfloat16)
        summed = summed + jnp.dot(onehot, piece, preferred_element_type=jnp.float32)
    gathered = summed.astype(jnp.bfloat16).reshape(2, tile_rows, width)

    def columns(rows, h, k):
        block = lax.dynamic_slice_in_dim(couplings, (h * 2 + k) * width, width, 2)
        return jnp.einsum("qtb,qbc->tc", rows, block, preferred_element_type=jnp.float32)

    far_in = lax.ppermute(columns(gathered, 1 - xh, 1 - c).astype(jnp.bfloat16), "c", SWAP)
    far = (columns(gathered, 1 - xh, c) + far_in.astype(jnp.float32)).astype(jnp.bfloat16)
    far, gathered = lax.optimization_barrier((far, gathered))
    far = lax.ppermute(far, "xh", SWAP)
    near_in = lax.ppermute(columns(gathered, xh, 1 - c).astype(jnp.bfloat16), "c", SWAP)
    numerators = columns(gathered, xh, c) + near_in.astype(jnp.float32) + far.astype(jnp.float32)
    energies = -(numerators * numerators) / energy_gap
    return (numerators, energies)


def solution(mesh):
    fine = Mesh(mesh.devices.reshape(SIZES), NAMES)
    ext, pair = EXT, NAMES[5:]
    in_specs = (
        P(ext, pair),
        P(ext, None),
        P(ext, None),
        P(ext, None),
        P(None, pair, None),
        P(ext, pair),
    )
    out_specs = (P(ext, pair), P(ext, pair))
    return jax.shard_map(shards, mesh=fine, in_specs=in_specs, out_specs=out_specs, check_vma=False)
```

```python
import jax
import jax.numpy as jnp
from jax import lax
from jax.experimental import pallas as pl
from jax.experimental.pallas import tpu as pltpu
from jax.sharding import Mesh
from jax.sharding import PartitionSpec as P

NAMES = ("xl", "zh", "zl", "yh", "yl", "xh", "c")
SIZES = (2, 6, 2, 4, 2, 2, 2)
EXT = NAMES[:5]
FAR = ("zh", "yh")
NEAR = ((1, 1), (1, 0), (0, 1))
SWAP = [(0, 1), (1, 0)]
STEP = 256


def shift(dx, dz, dy):
    pairs = []
    for x in range(2):
        for z in range(12):
            for y in range(8):
                for k in range(4):
                    s = 1 if k % 2 else -1
                    there = (((x + dx) % 2) * 12 + (z + s * dz) % 12) * 8 + (y + s * dy) % 8
                    pairs.append((((x * 12 + z) * 8 + y) * 4 + k, there * 4 + k))
    return pairs


def contract_kernel(starts, rows_ref, table_ref, out_ref, held, sems):
    parts, depth, width = out_ref.shape[0], rows_ref.shape[1], out_ref.shape[2]
    tile_rows = out_ref.shape[1]
    blocks = [(q, k) for q in range(table_ref.shape[0]) for k in range(depth // STEP)]
    copies = []
    for p in range(parts):
        start = pl.multiple_of(starts[p], 128)
        for at, (q, k) in enumerate(blocks):
            copy = pltpu.make_async_copy(
                table_ref.at[q, pl.ds(k * STEP, STEP), pl.ds(start, width)],
                held.at[p, at],
                sems.at[p, at],
            )
            copy.start()
            copies.append(copy)
    for p in range(parts):
        total = None
        for at, (q, k) in enumerate(blocks):
            copies[p * len(blocks) + at].wait()
            term = jnp.dot(
                rows_ref[q * tile_rows:(q + 1) * tile_rows, k * STEP:(k + 1) * STEP],
                held[p, at],
                preferred_element_type=jnp.float32,
            )
            total = term if total is None else total + term
        out_ref[p] = total.astype(out_ref.dtype)


def contract(rows, table, starts, kinds):
    blocks, depth, columns = table.shape
    parts, tile_rows, width = starts.shape[0], rows.shape[0] // blocks, rows.shape[1]
    count = blocks * (depth // STEP)
    return pl.pallas_call(
        contract_kernel,
        out_shape=[jax.ShapeDtypeStruct((parts, tile_rows, width), kind) for kind in kinds],
        in_specs=[
            pl.BlockSpec(memory_space=pltpu.SMEM),
            pl.BlockSpec(memory_space=pltpu.VMEM),
            pl.BlockSpec(memory_space=pl.ANY),
        ],
        out_specs=[pl.BlockSpec(memory_space=pltpu.VMEM) for _ in kinds],
        scratch_shapes=[
            pltpu.VMEM((parts, count, STEP, width), table.dtype),
            pltpu.SemaphoreType.DMA((parts, count)),
        ],
        compiler_params=pltpu.CompilerParams(vmem_limit_bytes=24 << 20),
        cost_estimate=pl.CostEstimate(
            flops=2 * parts * tile_rows * blocks * depth * width,
            bytes_accessed=2 * parts * blocks * depth * width,
            transcendentals=0,
        ),
    )(starts, rows, table)


def shards(core_coef, dest_rows, block_ids, bin_offsets, couplings, energy_gap):
    xl, zl, yl = lax.axis_index("xl"), lax.axis_index("zl"), lax.axis_index("yl")
    xh, c = lax.axis_index("xh"), lax.axis_index("c")
    group_rows, width = core_coef.shape
    tile_rows = energy_gap.shape[0]
    spread = jnp.broadcast_to(core_coef[None], (24, group_rows, width))
    own = lax.all_to_all(spread, FAR, 0, 0, tiled=True).reshape(192, width)
    beside = lax.ppermute(own, NAMES, shift(1, 0, 0))
    pieces = [((0, 0, 0), own)]
    pieces += [((0,) + at, lax.ppermute(own, NAMES, shift(0, *at))) for at in NEAR]
    pieces += [((1, 0, 0), beside)]
    pieces += [((1,) + at, lax.ppermute(beside, NAMES, shift(0, *at))) for at in NEAR]

    within = jnp.arange(8, dtype=jnp.int32)
    target = jnp.where(
        within[None, :] < bin_offsets[0][:, None],
        block_ids[0].reshape(192, 8) * tile_rows + dest_rows[0].reshape(192, 8),
        -1,
    )
    target = target.reshape(2, 6, 2, 4, 2, 8).transpose(0, 2, 4, 1, 3, 5).reshape(2, 2, 2, 192)
    slots = jnp.arange(2 * tile_rows, dtype=jnp.int32)
    summed = jnp.zeros((2 * tile_rows, width), jnp.float32)
    for (dx, dz, dy), piece in pieces:
        row = target[(xl + dx) % 2, (zl + dz) % 2, (yl + dy) % 2]
        onehot = (slots[:, None] == row[None, :]).astype(jnp.bfloat16)
        summed = summed + jnp.dot(onehot, piece, preferred_element_type=jnp.float32)
    gathered = summed.astype(jnp.bfloat16)

    far_out, near_out = (xh * -2 + 2 + 1 - c), (xh * 2 + 1 - c)
    far_own, near_own = (xh * -2 + 2 + c), (xh * 2 + c)
    out = contract(gathered, couplings, jnp.stack([far_out, near_out]) * width, (jnp.bfloat16,))
    beside_in = lax.ppermute(out[0], "c", SWAP)
    sums = contract(
        gathered, couplings, jnp.stack([far_own, near_own]) * width, (jnp.float32,)
    )[0]
    far = (sums[0] + beside_in[0].astype(jnp.float32)).astype(jnp.bfloat16)
    far_in = lax.ppermute(far, "xh", SWAP)
    numerators = sums[1] + beside_in[1].astype(jnp.float32) + far_in.astype(jnp.float32)
    energies = -(numerators * numerators) / energy_gap
    return (numerators, energies)


def solution(mesh):
    fine = Mesh(mesh.devices.reshape(SIZES), NAMES)
    ext, pair = EXT, NAMES[5:]
    in_specs = (
        P(ext, pair),
        P(ext, None),
        P(ext, None),
        P(ext, None),
        P(None, pair, None),
        P(ext, pair),
    )
    out_specs = (P(ext, pair), P(ext, pair))
    return jax.shard_map(shards, mesh=fine, in_specs=in_specs, out_specs=out_specs, check_vma=False)
```

```python
import jax
import jax.numpy as jnp
from jax import lax
from jax.experimental import pallas as pl
from jax.experimental.pallas import tpu as pltpu
from jax.sharding import Mesh
from jax.sharding import PartitionSpec as P

NAMES = ("xl", "zh", "zl", "yh", "yl", "xh", "c")
SIZES = (2, 6, 2, 4, 2, 2, 2)
EXT = NAMES[:5]
FAR = ("zh", "yh")
NEAR = ((0, 1), (1, 0), (1, 1))
SWAP = [(0, 1), (1, 0)]


def shift(dx, dz, dy):
    pairs = []
    for x in range(2):
        for z in range(12):
            for y in range(8):
                for k in range(4):
                    s = 1 if k % 2 else -1
                    there = (((x + dx) % 2) * 12 + (z + s * dz) % 12) * 8 + (y + s * dy) % 8
                    pairs.append((((x * 12 + z) * 8 + y) * 4 + k, there * 4 + k))
    return pairs


def contract_kernel(rows_ref, *refs):
    tables, out_ref = refs[:-1], refs[-1]
    tile_rows = out_ref.shape[1]
    for p, table_ref in enumerate(tables):
        total = None
        for q in range(table_ref.shape[0]):
            term = jnp.dot(
                rows_ref[q * tile_rows:(q + 1) * tile_rows, :],
                table_ref[q],
                preferred_element_type=jnp.float32,
            )
            total = term if total is None else total + term
        out_ref[p] = total.astype(out_ref.dtype)


def contract(rows, tables, kind):
    blocks, depth, width = tables[0].shape
    parts, tile_rows = len(tables), rows.shape[0] // blocks
    return pl.pallas_call(
        contract_kernel,
        out_shape=jax.ShapeDtypeStruct((parts, tile_rows, width), kind),
        in_specs=[pl.BlockSpec(memory_space=pltpu.VMEM) for _ in range(1 + parts)],
        out_specs=pl.BlockSpec(memory_space=pltpu.VMEM),
        compiler_params=pltpu.CompilerParams(vmem_limit_bytes=20 << 20),
        cost_estimate=pl.CostEstimate(
            flops=2 * parts * tile_rows * blocks * depth * width,
            bytes_accessed=2 * parts * blocks * depth * width,
            transcendentals=0,
        ),
    )(rows, *tables)


def shards(core_coef, dest_rows, block_ids, bin_offsets, couplings, energy_gap):
    xl, zl, yl = lax.axis_index("xl"), lax.axis_index("zl"), lax.axis_index("yl")
    xh, c = lax.axis_index("xh"), lax.axis_index("c")
    group_rows, width = core_coef.shape
    tile_rows = energy_gap.shape[0]
    spread = jnp.broadcast_to(core_coef[None], (24, group_rows, width))
    own = lax.all_to_all(spread, FAR, 0, 0, tiled=True).reshape(192, width)
    tables = [
        lax.dynamic_slice_in_dim(couplings, (h * 2 + k) * width, width, 2)
        for k in (1 - c, c)
        for h in (1 - xh, xh)
    ]
    own, tables = lax.optimization_barrier((own, tables))
    beside = lax.ppermute(own, NAMES, shift(1, 0, 0))
    pieces = [((0, 0, 0), own)]
    pieces += [((0,) + at, lax.ppermute(own, NAMES, shift(0, *at))) for at in NEAR]
    pieces += [((1, 0, 0), beside)]
    pieces += [((1,) + at, lax.ppermute(beside, NAMES, shift(0, *at))) for at in NEAR]

    within = jnp.arange(8, dtype=jnp.int32)
    target = jnp.where(
        within[None, :] < bin_offsets[0][:, None],
        block_ids[0].reshape(192, 8) * tile_rows + dest_rows[0].reshape(192, 8),
        -1,
    )
    target = target.reshape(2, 6, 2, 4, 2, 8).transpose(0, 2, 4, 1, 3, 5).reshape(2, 2, 2, 192)
    slots = jnp.arange(2 * tile_rows, dtype=jnp.int32)
    summed = jnp.zeros((2 * tile_rows, width), jnp.float32)
    for (dx, dz, dy), piece in pieces:
        row = target[(xl + dx) % 2, (zl + dz) % 2, (yl + dy) % 2]
        onehot = (slots[:, None] == row[None, :]).astype(jnp.bfloat16)
        summed = summed + jnp.dot(onehot, piece, preferred_element_type=jnp.float32)
    gathered = summed.astype(jnp.bfloat16)

    out = contract(gathered, tables[:2], jnp.bfloat16)
    beside_in = lax.ppermute(out, "c", SWAP)
    sums = contract(gathered, tables[2:], jnp.float32)
    far = (sums[0] + beside_in[0].astype(jnp.float32)).astype(jnp.bfloat16)
    far_in = lax.ppermute(far, "xh", SWAP)
    numerators = sums[1] + beside_in[1].astype(jnp.float32) + far_in.astype(jnp.float32)
    energies = -(numerators * numerators) / energy_gap
    return (numerators, energies)


def solution(mesh):
    fine = Mesh(mesh.devices.reshape(SIZES), NAMES)
    ext, pair = EXT, NAMES[5:]
    in_specs = (
        P(ext, pair),
        P(ext, None),
        P(ext, None),
        P(ext, None),
        P(None, pair, None),
        P(ext, pair),
    )
    out_specs = (P(ext, pair), P(ext, pair))
    return jax.shard_map(shards, mesh=fine, in_specs=in_specs, out_specs=out_specs, check_vma=False)
```

```python
import jax
import jax.numpy as jnp
from jax import lax
from jax.experimental import pallas as pl
from jax.experimental.pallas import tpu as pltpu
from jax.sharding import Mesh
from jax.sharding import PartitionSpec as P

NAMES = ("xl", "zh", "zl", "yh", "yl", "xh", "c")
SIZES = (2, 6, 2, 4, 2, 2, 2)
EXT = NAMES[:5]
FAR = ("zh", "yh")
NEAR = ((0, 1), (1, 0), (1, 1))
SWAP = [(0, 1), (1, 0)]


def shift(dx, dz, dy):
    pairs = []
    for x in range(2):
        for z in range(12):
            for y in range(8):
                for k in range(4):
                    s = 1 if k % 2 else -1
                    there = (((x + dx) % 2) * 12 + (z + s * dz) % 12) * 8 + (y - s * dy) % 8
                    pairs.append((((x * 12 + z) * 8 + y) * 4 + k, there * 4 + k))
    return pairs


def product(rows_ref, read, blocks, tile_rows):
    total = None
    for q in range(blocks):
        term = jnp.dot(
            rows_ref[q * tile_rows:(q + 1) * tile_rows, :],
            read(q),
            preferred_element_type=jnp.float32,
        )
        total = term if total is None else total + term
    return total


def columns_kernel(starts, rows_ref, table_ref, out_ref):
    parts, tile_rows, width = out_ref.shape
    for p in range(parts):
        at = pl.ds(pl.multiple_of(starts[p], 128), width)
        out = product(rows_ref, lambda q: table_ref[q, :, at], table_ref.shape[0], tile_rows)
        out_ref[p] = out.astype(out_ref.dtype)


def tables_kernel(rows_ref, *refs):
    tables, out_ref = refs[:-1], refs[-1]
    for p, table_ref in enumerate(tables):
        out = product(rows_ref, lambda q: table_ref[q], table_ref.shape[0], out_ref.shape[1])
        out_ref[p] = out.astype(out_ref.dtype)


def contract(kernel, starts, rows, tables, kind):
    blocks, depth, _ = tables[0].shape
    parts = len(tables) if starts is None else starts.shape[0]
    tile_rows, width = rows.shape[0] // blocks, rows.shape[1]
    scalars = [] if starts is None else [starts]
    return pl.pallas_call(
        kernel,
        out_shape=jax.ShapeDtypeStruct((parts, tile_rows, width), kind),
        in_specs=[pl.BlockSpec(memory_space=pltpu.SMEM) for _ in scalars]
        + [pl.BlockSpec(memory_space=pltpu.VMEM) for _ in range(1 + len(tables))],
        out_specs=pl.BlockSpec(memory_space=pltpu.VMEM),
        compiler_params=pltpu.CompilerParams(vmem_limit_bytes=20 << 20),
        cost_estimate=pl.CostEstimate(
            flops=2 * parts * tile_rows * blocks * depth * width,
            bytes_accessed=2 * parts * blocks * depth * width,
            transcendentals=0,
        ),
    )(*scalars, rows, *tables)


def shards(core_coef, dest_rows, block_ids, bin_offsets, couplings, energy_gap):
    xl, zl, yl = lax.axis_index("xl"), lax.axis_index("zl"), lax.axis_index("yl")
    xh, c = lax.axis_index("xh"), lax.axis_index("c")
    group_rows, width = core_coef.shape
    tile_rows = energy_gap.shape[0]
    spread = jnp.broadcast_to(core_coef[None], (24, group_rows, width))
    own = lax.all_to_all(spread, FAR, 0, 0, tiled=True).reshape(192, width)
    tables = [
        lax.dynamic_slice_in_dim(couplings, (h * 2 + c) * width, width, 2) for h in (1 - xh, xh)
    ]
    own, tables = lax.optimization_barrier((own, tables))
    beside = lax.ppermute(own, NAMES, shift(1, 0, 0))
    across = [lax.ppermute(own, NAMES, shift(0, *at)) for at in NEAR]
    pieces = [((0, 0, 0), own)] + [((0,) + at, piece) for at, piece in zip(NEAR, across)]
    pieces += [((1, 0, 0), beside)]
    pieces += [((1,) + at, lax.ppermute(beside, NAMES, shift(0, *at))) for at in NEAR[:2]]
    pieces += [((1,) + NEAR[2], lax.ppermute(across[2], NAMES, shift(1, 0, 0)))]

    within = jnp.arange(8, dtype=jnp.int32)
    target = jnp.where(
        within[None, :] < bin_offsets[0][:, None],
        block_ids[0].reshape(192, 8) * tile_rows + dest_rows[0].reshape(192, 8),
        -1,
    )
    target = target.reshape(2, 6, 2, 4, 2, 8).transpose(0, 2, 4, 1, 3, 5).reshape(2, 2, 2, 192)
    slots = jnp.arange(2 * tile_rows, dtype=jnp.int32)
    summed = jnp.zeros((2 * tile_rows, width), jnp.float32)
    for (dx, dz, dy), piece in pieces:
        row = target[(xl + dx) % 2, (zl + dz) % 2, (yl + dy) % 2]
        onehot = (slots[:, None] == row[None, :]).astype(jnp.bfloat16)
        summed = summed + jnp.dot(onehot, piece, preferred_element_type=jnp.float32)
    gathered = summed.astype(jnp.bfloat16)

    starts = jnp.stack([(h * 2 + 1 - c) * width for h in (1 - xh, xh)])
    out = contract(columns_kernel, starts, gathered, [couplings], jnp.bfloat16)
    beside_in = lax.ppermute(out, "c", SWAP)
    sums = contract(tables_kernel, None, gathered, tables, jnp.float32)
    far = (sums[0] + beside_in[0].astype(jnp.float32)).astype(jnp.bfloat16)
    far_in = lax.ppermute(far, "xh", SWAP)
    numerators = sums[1] + beside_in[1].astype(jnp.float32) + far_in.astype(jnp.float32)
    energies = -(numerators * numerators) / energy_gap
    return (numerators, energies)


def solution(mesh):
    fine = Mesh(mesh.devices.reshape(SIZES), NAMES)
    ext, pair = EXT, NAMES[5:]
    in_specs = (
        P(ext, pair),
        P(ext, None),
        P(ext, None),
        P(ext, None),
        P(None, pair, None),
        P(ext, pair),
    )
    out_specs = (P(ext, pair), P(ext, pair))
    return jax.shard_map(shards, mesh=fine, in_specs=in_specs, out_specs=out_specs, check_vma=False)
```

```python
import jax
import jax.numpy as jnp
from jax import lax
from jax.experimental import pallas as pl
from jax.experimental.pallas import tpu as pltpu
from jax.sharding import Mesh
from jax.sharding import PartitionSpec as P

NAMES = ("xl", "zh", "zl", "yh", "yl", "xh", "c")
SIZES = (2, 6, 2, 4, 2, 2, 2)
EXT = NAMES[:5]
FAR = ("zh", "yh")
NEAR = ((0, 1), (1, 0), (1, 1))
SWAP = [(0, 1), (1, 0)]


def shift(dx, dz, dy):
    pairs = []
    for x in range(2):
        for z in range(12):
            for y in range(8):
                for k in range(4):
                    s = 1 if k % 2 else -1
                    there = (((x + dx) % 2) * 12 + (z + s * dz) % 12) * 8 + (y - s * dy) % 8
                    pairs.append((((x * 12 + z) * 8 + y) * 4 + k, there * 4 + k))
    return pairs


def product(rows_ref, read, blocks, tile_rows):
    total = None
    for q in range(blocks):
        term = jnp.dot(
            rows_ref[q * tile_rows:(q + 1) * tile_rows, :],
            read(q),
            preferred_element_type=jnp.float32,
        )
        total = term if total is None else total + term
    return total


def columns_kernel(starts, rows_ref, table_ref, out_ref):
    parts, tile_rows, width = out_ref.shape
    for p in range(parts):
        at = pl.ds(pl.multiple_of(starts[p], 128), width)
        out = product(rows_ref, lambda q: table_ref[q, :, at], table_ref.shape[0], tile_rows)
        out_ref[p] = out.astype(out_ref.dtype)


def tables_kernel(rows_ref, *refs):
    tables, out_ref = refs[:-1], refs[-1]
    for p, table_ref in enumerate(tables):
        out = product(rows_ref, lambda q: table_ref[q], table_ref.shape[0], out_ref.shape[1])
        out_ref[p] = out.astype(out_ref.dtype)


def contract(kernel, starts, rows, tables, kind):
    blocks, depth, _ = tables[0].shape
    parts = len(tables) if starts is None else starts.shape[0]
    tile_rows, width = rows.shape[0] // blocks, rows.shape[1]
    scalars = [] if starts is None else [starts]
    return pl.pallas_call(
        kernel,
        out_shape=jax.ShapeDtypeStruct((parts, tile_rows, width), kind),
        in_specs=[pl.BlockSpec(memory_space=pltpu.SMEM) for _ in scalars]
        + [pl.BlockSpec(memory_space=pltpu.VMEM) for _ in range(1 + len(tables))],
        out_specs=pl.BlockSpec(memory_space=pltpu.VMEM),
        compiler_params=pltpu.CompilerParams(vmem_limit_bytes=20 << 20),
        cost_estimate=pl.CostEstimate(
            flops=2 * parts * tile_rows * blocks * depth * width,
            bytes_accessed=2 * parts * blocks * depth * width,
            transcendentals=0,
        ),
    )(*scalars, rows, *tables)


def shards(core_coef, dest_rows, block_ids, bin_offsets, couplings, energy_gap):
    xl, zl, yl = lax.axis_index("xl"), lax.axis_index("zl"), lax.axis_index("yl")
    xh, c = lax.axis_index("xh"), lax.axis_index("c")
    group_rows, width = core_coef.shape
    tile_rows = energy_gap.shape[0]
    spread = jnp.broadcast_to(core_coef[None], (24, group_rows, width))
    own = lax.all_to_all(spread, FAR, 0, 0, tiled=True).reshape(192, width)
    tables = [
        lax.dynamic_slice_in_dim(couplings, (h * 2 + c) * width, width, 2) for h in (1 - xh, xh)
    ]
    own, tables[0] = lax.optimization_barrier((own, tables[0]))
    beside = lax.ppermute(own, NAMES, shift(1, 0, 0))
    across = [lax.ppermute(own, NAMES, shift(0, *at)) for at in NEAR]
    pieces = [((0, 0, 0), own)] + [((0,) + at, piece) for at, piece in zip(NEAR, across)]
    pieces += [((1, 0, 0), beside)]
    pieces += [((1,) + at, lax.ppermute(beside, NAMES, shift(0, *at))) for at in NEAR[:2]]
    pieces += [((1,) + NEAR[2], lax.ppermute(across[2], NAMES, shift(1, 0, 0)))]

    at, piece = pieces[-2]
    piece, tables[1] = lax.optimization_barrier((piece, tables[1]))
    pieces[-2] = (at, piece)

    within = jnp.arange(8, dtype=jnp.int32)
    target = jnp.where(
        within[None, :] < bin_offsets[0][:, None],
        block_ids[0].reshape(192, 8) * tile_rows + dest_rows[0].reshape(192, 8),
        -1,
    )
    target = target.reshape(2, 6, 2, 4, 2, 8).transpose(0, 2, 4, 1, 3, 5).reshape(2, 2, 2, 192)
    slots = jnp.arange(2 * tile_rows, dtype=jnp.int32)
    summed = jnp.zeros((2 * tile_rows, width), jnp.float32)
    for (dx, dz, dy), piece in pieces:
        row = target[(xl + dx) % 2, (zl + dz) % 2, (yl + dy) % 2]
        onehot = (slots[:, None] == row[None, :]).astype(jnp.bfloat16)
        summed = summed + jnp.dot(onehot, piece, preferred_element_type=jnp.float32)
    gathered = summed.astype(jnp.bfloat16)

    starts = jnp.stack([(h * 2 + 1 - c) * width for h in (1 - xh, xh)])
    out = contract(columns_kernel, starts, gathered, [couplings], jnp.bfloat16)
    beside_in = lax.ppermute(out, "c", SWAP)
    sums = contract(tables_kernel, None, gathered, tables, jnp.float32)
    far = (sums[0] + beside_in[0].astype(jnp.float32)).astype(jnp.bfloat16)
    far_in = lax.ppermute(far, "xh", SWAP)
    numerators = sums[1] + beside_in[1].astype(jnp.float32) + far_in.astype(jnp.float32)
    energies = -(numerators * numerators) / energy_gap
    return (numerators, energies)


def solution(mesh):
    fine = Mesh(mesh.devices.reshape(SIZES), NAMES)
    ext, pair = EXT, NAMES[5:]
    in_specs = (
        P(ext, pair),
        P(ext, None),
        P(ext, None),
        P(ext, None),
        P(None, pair, None),
        P(ext, pair),
    )
    out_specs = (P(ext, pair), P(ext, pair))
    return jax.shard_map(shards, mesh=fine, in_specs=in_specs, out_specs=out_specs, check_vma=False)
```
